32 devices in a mesh: comp: 8 (over y, x, core), pair: 4 (over z).
Axes of the slice: x: 2, y: 2, z: 4, core: 2. Of those that a mesh axis runs over, the one named last changes fastest.
Arguments:
- densities: bfloat16 [8192, 16384], P('comp', 'pair'), may hold values from -6 to 6
- coulomb: float32 [8192], replicated, may hold values from 3.314563e-05 to 0.003314563
- pair_list: int32 [256, 2], P(('comp', 'pair')), may hold values from 0 to 4095
- valence_energy: float32 [4096], replicated, may hold values from -20 to -0.5, as said below
- conduction_energy: float32 [4096], replicated, may hold values from 0.5 to 12, as said below
- tile_mask: int32 [128, 8], P(('pair', 'comp')), may hold values 0 or 1
Outputs:
- kernel: float32 [16384, 256], P(('pair', 'comp'))
The draws below stay inside these ranges and needn't reach their ends.
Inputs may be any that keep to these rules, and one draw needn't show every extreme that they name: `valence_energy`: energies in electronvolts. `conduction_energy`: energies in electronvolts.
All inputs are finite; a program needn't handle non-finite values. No bound on the sum of `tile_mask` on one device may be relied on, other than what follows from the above.
Results may differ from the reference program's by a relative error of at most 0.0025.
Values may be sent and summed in bfloat16 or wider, within the bound.
A program may use at most 128 MiB of HBM per device.

```python
import math
import jax
import jax.numpy as jnp
from jax import lax

NG = 8192
NWAN = 4096
TILE = 128
PAIR_DEV = 512
ROW_DEV = 8
NPAIR = 16384
ROWS = 256
N_COMP = 8
N_PAIR = 4


def draw_valence_energy(key, part):
    level = jax.random.uniform(jax.random.fold_in(key, 11), (NWAN,), jnp.float32)
    return -0.5 - 19.5 * level


def draw_conduction_energy(key, part):
    level = jax.random.uniform(jax.random.fold_in(key, 23), (NWAN,), jnp.float32)
    return 0.5 + 11.5 * level


def place_ends(array, rng, low, largest):
    dims = array.shape
    spot = [jax.random.randint(jax.random.fold_in(rng, axis), (), 0, dims[axis]) for axis in range(len(dims))]
    array = array.at[tuple(spot)].set(low)
    longest = dims.index(max(dims))
    spot[longest] = (spot[longest] + 1) % dims[longest]
    return array.at[tuple(spot)].set(largest)


def block_scale(own_key, dims, cuts, smallest, largest):
    level = 1.0
    for axis_at, parts in cuts:
        steps = jax.random.uniform(jax.random.fold_in(jax.random.fold_in(own_key, 6), axis_at), (parts,), jnp.float32, smallest / len(cuts), largest / len(cuts))
        level = level * jnp.repeat(jnp.exp(steps), dims[axis_at] // parts).reshape((-1,) + (1,) * (len(dims) - 1 - axis_at))
    return level


def gaussian(stream_key, dims, scale, limit, split=(), kind=jnp.bfloat16):
    values = scale * jax.random.normal(stream_key, dims, jnp.float32)
    if split:
        values = values * block_scale(stream_key, dims, split, -0.22, 0.18)
    return jnp.clip(values, -limit, limit).astype(kind)


def setup_inputs(seed: int = 0) -> dict:
    seeds = jax.random.split(jax.random.key(seed), 7)
    densities = gaussian(seeds[0], (NG, NPAIR), 1.0, 6.0, ((0, 8), (1, 4)))
    coulomb = jnp.clip(jnp.exp(jax.random.uniform(seeds[1], (NG,), jnp.float32, math.log(3.3145628549391404e-05), math.log(0.003314563))), 3.3145628549391404e-05, 0.003314563)
    pair_list = place_ends(jax.random.randint(seeds[2], (ROWS, 2), 0, NWAN), jax.random.fold_in(seeds[2], 1), 0, NWAN - 1).astype(jnp.int32)
    valence_energy = draw_valence_energy(jax.random.fold_in(seeds[6], 71), 0)
    conduction_energy = draw_conduction_energy(jax.random.fold_in(seeds[6], 71), 0)
    tile_mask = place_ends((jax.random.randint(seeds[5], (NPAIR // TILE, N_COMP), 0, 4) < 3).astype(jnp.int32), jax.random.fold_in(seeds[5], 1), 0, 1)
    return dict(densities=densities, coulomb=coulomb, pair_list=pair_list, valence_energy=valence_energy, conduction_energy=conduction_energy, tile_mask=tile_mask)


def reference(densities, coulomb, pair_list, valence_energy, conduction_energy, tile_mask):
    blocks = densities.reshape(NG, N_PAIR, N_COMP, PAIR_DEV)[:, :, :, :ROW_DEV]
    rows = jnp.transpose(blocks, (2, 1, 3, 0)).reshape(ROWS, NG)
    panel = (rows.astype(jnp.float32) * coulomb[None, :]).astype(jnp.bfloat16)
    exchange = lax.dot_general(densities, panel, (((0,), (1,)), ((), ())), preferred_element_type=jnp.float32)
    masked = exchange.reshape(NPAIR // TILE, TILE, N_COMP, ROWS // N_COMP) * tile_mask.astype(jnp.float32)[:, None, :, None]
    masked = 2.0 * masked.reshape(NPAIR, ROWS)
    energy = conduction_energy[pair_list[:, 1]] - valence_energy[pair_list[:, 0]]
    index = jnp.arange(ROWS, dtype=jnp.int32)
    blk_c = index // (N_PAIR * ROW_DEV)
    blk_p = (index // ROW_DEV) % N_PAIR
    inner = index % ROW_DEV
    owner = (blk_p * N_COMP + blk_c) * PAIR_DEV + inner
    return masked.at[owner, index].add(energy)
```

```python
import functools

import jax
import jax.numpy as jnp
from jax import lax
from jax.experimental import pallas as pl
from jax.experimental.pallas import tpu as pltpu
from jax.sharding import PartitionSpec as P

TILE = 128
LANES = 128
MESH = pl.DeviceIdType.MESH
F32 = jnp.float32
BF16 = jnp.bfloat16


def xor(a, b, bits):
    out = 0
    for i in range(bits):
        x, y = (a // 2**i) % 2, (b // 2**i) % 2
        out = out + 2**i * (x + y - 2 * x * y)
    return out


def kernel(
    comps, pairs, row_dev,
    d_hbm, w_ref, list_ref, val_ref, cond_ref, mask_ref, out_ref,
    d_v, panel, own, core_out, core_in, chip_out, chip_in, acc,
    load_sem, pan_s, pan_r, core_s, core_r, chip_s, chip_r,
):
    c = lax.axis_index("comp")
    p = lax.axis_index("pair")
    chips = comps // 2
    chip_bits = chips.bit_length() - 1
    pair_bits = pairs.bit_length() - 1
    core, chip = c % 2, c // 2
    block_len = d_v.shape[0]
    width = d_v.shape[1] // comps
    rows = comps * row_dev
    window = pairs * rows

    def chip_at(m):
        return xor(chip, m, chip_bits)

    spans = [(b * width, LANES) for b in range(comps)]
    spans += [(b * width + LANES, width - LANES) for b in range(comps)]
    loads = [
        pltpu.make_async_copy(
            d_hbm.at[:, pl.ds(at, size)], d_v.at[:, pl.ds(at, size)], load_sem.at[i]
        )
        for i, (at, size) in enumerate(spans)
    ]
    for load in loads:
        load.start()

    barrier = pltpu.get_barrier_semaphore()
    peers = [{"comp": 2 * chip + 1 - core, "pair": p}]
    peers += [{"comp": 2 * chip_at(m) + core, "pair": p} for m in range(1, chips)]
    peers += [{"comp": c, "pair": xor(p, k, pair_bits)} for k in range(1, pairs)]
    for peer in peers:
        pl.semaphore_signal(barrier, inc=1, device_id=peer, device_id_type=MESH)

    for load in loads[:comps]:
        load.wait()
    shape = (rows, comps * LANES)
    row = lax.broadcasted_iota(jnp.int32, shape, 0)
    col = lax.broadcasted_iota(jnp.int32, shape, 1)
    select = ((row // row_dev) * LANES + row % row_dev == col).astype(F32).astype(BF16)
    picked = jnp.concatenate([d_v[:, b * width : b * width + LANES] for b in range(comps)], axis=1)
    turned = lax.dot_general(select, picked, (((1,), (1,)), ((), ())), preferred_element_type=F32)
    per = block_len // LANES
    for i in range(per):
        cols = slice(i * LANES, (i + 1) * LANES)
        panel[p, :, cols] = (turned[:, cols] * w_ref[pl.ds(c * per + i, 1), :]).astype(BF16)

    pl.semaphore_wait(barrier, len(peers))

    def panel_copy(k, source):
        return pltpu.make_async_remote_copy(
            src_ref=panel.at[source],
            dst_ref=panel.at[source],
            send_sem=pan_s.at[k - 1],
            recv_sem=pan_r.at[k - 1],
            device_id={"comp": c, "pair": xor(p, k, pair_bits)},
            device_id_type=MESH,
        )

    for k in range(1, pairs):
        panel_copy(k, p).start()

    def core_copy(k, m):
        return pltpu.make_async_remote_copy(
            src_ref=core_out.at[k, m],
            dst_ref=core_in.at[k, m],
            send_sem=core_s.at[k, m],
            recv_sem=core_r.at[k, m],
            device_id={"comp": 2 * chip + 1 - core, "pair": p},
            device_id_type=MESH,
        )

    def chip_copy(k, m):
        return pltpu.make_async_remote_copy(
            src_ref=chip_out.at[k, m - 1],
            dst_ref=chip_in.at[k, m - 1],
            send_sem=chip_s.at[k, m - 1],
            recv_sem=chip_r.at[k, m - 1],
            device_id={"comp": 2 * chip_at(m) + core, "pair": p},
            device_id_type=MESH,
        )

    table = val_ref.shape
    place = lax.broadcasted_iota(jnp.int32, table, 0) * LANES
    place = place + lax.broadcasted_iota(jnp.int32, table, 1)
    tile = (row_dev, LANES)
    on_row = lax.broadcasted_iota(jnp.int32, tile, 0)
    on_col = lax.broadcasted_iota(jnp.int32, tile, 1)
    diagonal = jnp.zeros(tile, F32)
    for j in range(row_dev):
        up = jnp.where(place == list_ref[j, 1], cond_ref[...], 0.0)
        down = jnp.where(place == list_ref[j, 0], val_ref[...], 0.0)
        energy = jnp.sum(up, axis=(0, 1), keepdims=True) - jnp.sum(down, axis=(0, 1), keepdims=True)
        diagonal = jnp.where((on_row == j) & (on_col == j), energy, diagonal)

    for load in loads[comps:]:
        load.wait()

    def block(lhs, b):
        start = pl.multiple_of(b * width, width)
        return jnp.dot(lhs, d_v[:, pl.ds(start, width)], preferred_element_type=F32)

    def reduce(k):
        s = xor(p, k, pair_bits)
        total = own[k]
        for m in range(1, chips):
            chip_copy(k, m).wait_recv()
            total = total + chip_in[k, m - 1].astype(F32)
        for b in range(comps):
            at = pl.ds(pl.multiple_of((b * pairs + s) * row_dev, row_dev), row_dev)
            for t in range(width // TILE):
                cols = slice(t * TILE, (t + 1) * TILE)
                factor = 2.0 * mask_ref[t, b].astype(F32)
                acc[at, cols] = total[b * row_dev : (b + 1) * row_dev, cols] * factor

    def phase(k, carry):
        s = xor(p, k, pair_bits)

        @pl.when(k > 0)
        def _():
            panel_copy(k, s).wait_recv()

        lhs = panel[s]
        order = list(range(1, chips)) + [0]
        for m in order:
            core_out[k, m] = block(lhs, 2 * chip_at(m) + 1 - core).astype(BF16)
            core_copy(k, m).start()
        for m in order:
            part = block(lhs, 2 * chip_at(m) + core)
            core_copy(k, m).wait_recv()
            part = part + core_in[k, m].astype(F32)
            if m:
                chip_out[k, m - 1] = part.astype(BF16)
                chip_copy(k, m).start()
            else:
                own[k] = part

        @pl.when(k > 0)
        def _():
            reduce(k - 1)

        return carry

    lax.fori_loop(0, pairs, phase, 0)
    reduce(pairs - 1)

    at = pl.ds(pl.multiple_of((c * pairs + p) * row_dev, row_dev), row_dev)
    acc[at, :LANES] = acc[at, :LANES] + diagonal
    out_ref[...] = acc[...].T

    for k in range(1, pairs):
        panel_copy(k, p).wait_send()

    def drain(k, carry):
        for m in range(chips):
            core_copy(k, m).wait_send()
            if m:
                chip_copy(k, m).wait_send()
        return carry

    lax.fori_loop(0, pairs, drain, 0)


def per_device(densities, coulomb, pair_list, valence_energy, conduction_energy, tile_mask):
    comps = lax.axis_size("comp")
    pairs = lax.axis_size("pair")
    chips = comps // 2
    block_len, columns = densities.shape
    width = columns // comps
    row_dev = pair_list.shape[0]
    rows = comps * row_dev
    window = rows * pairs
    dma = pltpu.SemaphoreType.DMA
    vmem = pl.BlockSpec(memory_space=pltpu.VMEM)
    smem = pl.BlockSpec(memory_space=pltpu.SMEM)
    return pl.pallas_call(
        functools.partial(kernel, comps, pairs, row_dev),
        out_shape=jax.ShapeDtypeStruct((width, window), F32),
        in_specs=[pl.BlockSpec(memory_space=pl.ANY), vmem, smem, vmem, vmem, smem],
        out_specs=vmem,
        scratch_shapes=[
            pltpu.VMEM((block_len, columns), BF16),
            pltpu.VMEM((pairs, rows, block_len), BF16),
            pltpu.VMEM((pairs, rows, width), F32),
            pltpu.VMEM((pairs, chips, rows, width), BF16),
            pltpu.VMEM((pairs, chips, rows, width), BF16),
            pltpu.VMEM((pairs, chips - 1, rows, width), BF16),
            pltpu.VMEM((pairs, chips - 1, rows, width), BF16),
            pltpu.VMEM((window, width), F32),
            dma((2 * comps,)),
            dma((pairs - 1,)),
            dma((pairs - 1,)),
            dma((pairs, chips)),
            dma((pairs, chips)),
            dma((pairs, chips - 1)),
            dma((pairs, chips - 1)),
        ],
        compiler_params=pltpu.CompilerParams(
            collective_id=0, has_side_effects=True, vmem_limit_bytes=56 * 2**20
        ),
        cost_estimate=pl.CostEstimate(
            flops=2 * block_len * columns * window,
            bytes_accessed=2 * block_len * columns + 4 * width * window,
            transcendentals=0,
        ),
    )(
        densities,
        coulomb.reshape(-1, LANES),
        pair_list,
        valence_energy.reshape(-1, LANES),
        conduction_energy.reshape(-1, LANES),
        tile_mask,
    )


def solution(mesh):
    return jax.shard_map(
        per_device,
        mesh=mesh,
        in_specs=(
            P("comp", "pair"),
            P(),
            P(("comp", "pair"), None),
            P(),
            P(),
            P(("pair", "comp"), None),
        ),
        out_specs=P(("pair", "comp"), None),
        check_vma=False,
    )
```

```python
import functools

import jax
import jax.numpy as jnp
from jax import lax
from jax.experimental import pallas as pl
from jax.experimental.pallas import tpu as pltpu
from jax.sharding import PartitionSpec as P

TILE = 128
LANES = 128
GROUP = 2
MESH = pl.DeviceIdType.MESH
F32 = jnp.float32
BF16 = jnp.bfloat16


def xor(a, b, bits):
    out = 0
    for i in range(bits):
        x, y = (a // 2**i) % 2, (b // 2**i) % 2
        out = out + 2**i * (x + y - 2 * x * y)
    return out


def kernel(
    comps, pairs, row_dev, group,
    d_hbm, w_hbm, list_hbm, val_hbm, cond_hbm, mask_hbm, out_hbm,
    d_v, w_ref, list_ref, val_ref, cond_ref, mask_ref,
    panel, own, core_out, core_in, chip_out, chip_in, acc, out_v,
    load_sem, small_sem, out_sem, pan_s, pan_r, core_s, core_r, chip_s, chip_r,
):
    c = lax.axis_index("comp")
    p = lax.axis_index("pair")
    chips = comps // 2
    chip_bits = chips.bit_length() - 1
    pair_bits = pairs.bit_length() - 1
    core, chip = c % 2, c // 2
    block_len = d_v.shape[0]
    width = d_v.shape[1] // comps
    rows = comps * row_dev
    groups = pairs // group

    def chip_at(m):
        return xor(chip, m, chip_bits)

    spans = [(b * width, LANES) for b in range(comps)]
    spans += [(b * width + LANES, width - LANES) for b in range(comps)]
    loads = [
        pltpu.make_async_copy(
            d_hbm.at[:, pl.ds(at, size)], d_v.at[:, pl.ds(at, size)], load_sem.at[i]
        )
        for i, (at, size) in enumerate(spans)
    ]
    small = [
        pltpu.make_async_copy(source, target, small_sem.at[i])
        for i, (source, target) in enumerate(
            [
                (w_hbm, w_ref),
                (list_hbm, list_ref),
                (val_hbm, val_ref),
                (cond_hbm, cond_ref),
                (mask_hbm, mask_ref),
            ]
        )
    ]
    for load in loads[:comps] + small + loads[comps:]:
        load.start()

    barrier = pltpu.get_barrier_semaphore()
    peers = [{"comp": 2 * chip + 1 - core, "pair": p}]
    peers += [{"comp": 2 * chip_at(m) + core, "pair": p} for m in range(1, chips)]
    peers += [{"comp": c, "pair": xor(p, k, pair_bits)} for k in range(1, pairs)]
    for peer in peers:
        pl.semaphore_signal(barrier, inc=1, device_id=peer, device_id_type=MESH)

    shape = (rows, comps * LANES)
    row = lax.broadcasted_iota(jnp.int32, shape, 0)
    col = lax.broadcasted_iota(jnp.int32, shape, 1)
    select = ((row // row_dev) * LANES + row % row_dev == col).astype(F32).astype(BF16)
    for load in loads[:comps] + small[:1]:
        load.wait()
    picked = jnp.concatenate([d_v[:, b * width : b * width + LANES] for b in range(comps)], axis=1)
    turned = lax.dot_general(select, picked, (((1,), (1,)), ((), ())), preferred_element_type=F32)
    per = block_len // LANES
    for i in range(per):
        cols = slice(i * LANES, (i + 1) * LANES)
        panel[0, :, cols] = (turned[:, cols] * w_ref[pl.ds(c * per + i, 1), :]).astype(BF16)

    pl.semaphore_wait(barrier, len(peers))

    def panel_copy(k):
        return pltpu.make_async_remote_copy(
            src_ref=panel.at[0],
            dst_ref=panel.at[k],
            send_sem=pan_s.at[k - 1],
            recv_sem=pan_r.at[k - 1],
            device_id={"comp": c, "pair": xor(p, k, pair_bits)},
            device_id_type=MESH,
        )

    for k in range(1, pairs):
        panel_copy(k).start()

    def core_copy(g, m):
        return pltpu.make_async_remote_copy(
            src_ref=core_out.at[g, m],
            dst_ref=core_in.at[g, m],
            send_sem=core_s.at[g, m],
            recv_sem=core_r.at[g, m],
            device_id={"comp": 2 * chip + 1 - core, "pair": p},
            device_id_type=MESH,
        )

    def chip_copy(g, m):
        return pltpu.make_async_remote_copy(
            src_ref=chip_out.at[g, m - 1],
            dst_ref=chip_in.at[g, m - 1],
            send_sem=chip_s.at[g, m - 1],
            recv_sem=chip_r.at[g, m - 1],
            device_id={"comp": 2 * chip_at(m) + core, "pair": p},
            device_id_type=MESH,
        )

    for load in small[1:]:
        load.wait()
    table = val_ref.shape
    place = lax.broadcasted_iota(jnp.int32, table, 0) * LANES
    place = place + lax.broadcasted_iota(jnp.int32, table, 1)
    tile = (row_dev, LANES)
    on_row = lax.broadcasted_iota(jnp.int32, tile, 0)
    on_col = lax.broadcasted_iota(jnp.int32, tile, 1)
    diagonal = jnp.zeros(tile, F32)
    for j in range(row_dev):
        up = jnp.where(place == list_ref[1, j], cond_ref[...], 0.0)
        down = jnp.where(place == list_ref[0, j], val_ref[...], 0.0)
        energy = jnp.sum(up, axis=(0, 1), keepdims=True) - jnp.sum(down, axis=(0, 1), keepdims=True)
        diagonal = jnp.where((on_row == j) & (on_col == j), energy, diagonal)

    for load in loads[comps:]:
        load.wait()

    def block(lhs, b):
        start = pl.multiple_of(b * width, width)
        return jnp.dot(lhs, d_v[:, pl.ds(start, width)], preferred_element_type=F32)

    def reduce(g):
        total = own[g]
        for m in range(1, chips):
            chip_copy(g, m).wait_recv()
            total = total + chip_in[g, m - 1].astype(F32)
        for i in range(group):
            s = xor(p, g * group + i, pair_bits)
            for b in range(comps):
                at = pl.ds(pl.multiple_of((b * pairs + s) * row_dev, row_dev), row_dev)
                first = i * rows + b * row_dev
                for t in range(width // TILE):
                    cols = slice(t * TILE, (t + 1) * TILE)
                    factor = 2.0 * mask_ref[t, b].astype(F32)
                    acc[at, cols] = total[first : first + row_dev, cols] * factor

    order = list(range(chips - 1, 0, -1)) + [0]
    steps = [(m, True) for m in order[:2]]
    for i, m in enumerate(order):
        steps.append((m, False))
        if i + 2 < chips:
            steps.append((order[i + 2], True))

    def phase(g, carry):
        for i in range(group):
            if i:
                panel_copy(g * group + i).wait_recv()
            else:

                @pl.when(g > 0)
                def _():
                    panel_copy(g * group).wait_recv()

        lhs = panel[pl.ds(g * group, group)].reshape(group * rows, block_len)
        for m, away in steps:
            if away:
                core_out[g, m] = block(lhs, 2 * chip_at(m) + 1 - core).astype(BF16)
                core_copy(g, m).start()
                continue
            part = block(lhs, 2 * chip_at(m) + core)
            core_copy(g, m).wait_recv()
            part = part + core_in[g, m].astype(F32)
            if m:
                chip_out[g, m - 1] = part.astype(BF16)
                chip_copy(g, m).start()
            else:
                own[g] = part

        @pl.when(g > 0)
        def _():
            reduce(g - 1)

        return carry

    lax.fori_loop(0, groups, phase, 0)
    reduce(groups - 1)

    at = pl.ds(pl.multiple_of((c * pairs + p) * row_dev, row_dev), row_dev)
    acc[at, :LANES] = acc[at, :LANES] + diagonal
    stores = []
    for t in range(width // TILE):
        cut = pl.ds(t * TILE, TILE)
        out_v[cut, :] = acc[:, t * TILE : (t + 1) * TILE].T
        stores.append(pltpu.make_async_copy(out_v.at[cut], out_hbm.at[cut], out_sem.at[t]))
        stores[-1].start()

    for k in range(1, pairs):
        panel_copy(k).wait_send()

    def drain(g, carry):
        for m in range(chips):
            core_copy(g, m).wait_send()
            if m:
                chip_copy(g, m).wait_send()
        return carry

    lax.fori_loop(0, groups, drain, 0)
    for store in stores:
        store.wait()


def per_device(densities, coulomb, pair_list, valence_energy, conduction_energy, tile_mask):
    comps = lax.axis_size("comp")
    pairs = lax.axis_size("pair")
    chips = comps // 2
    block_len, columns = densities.shape
    width = columns // comps
    row_dev = pair_list.shape[0]
    rows = comps * row_dev
    window = rows * pairs
    group = GROUP
    groups = pairs // group
    dma = pltpu.SemaphoreType.DMA
    operands = (
        densities,
        coulomb.reshape(-1, LANES),
        pair_list.T,
        valence_energy.reshape(-1, LANES),
        conduction_energy.reshape(-1, LANES),
        tile_mask,
    )
    _, w, pair, val, cond, mask = operands
    return pl.pallas_call(
        functools.partial(kernel, comps, pairs, row_dev, group),
        out_shape=jax.ShapeDtypeStruct((width, window), F32),
        in_specs=[pl.BlockSpec(memory_space=pl.ANY)] * 6,
        out_specs=pl.BlockSpec(memory_space=pl.ANY),
        scratch_shapes=[
            pltpu.VMEM((block_len, columns), BF16),
            pltpu.VMEM(w.shape, F32),
            pltpu.SMEM(pair.shape, jnp.int32),
            pltpu.VMEM(val.shape, F32),
            pltpu.VMEM(cond.shape, F32),
            pltpu.SMEM(mask.shape, jnp.int32),
            pltpu.VMEM((pairs, rows, block_len), BF16),
            pltpu.VMEM((groups, group * rows, width), F32),
            pltpu.VMEM((groups, chips, group * rows, width), BF16),
            pltpu.VMEM((groups, chips, group * rows, width), BF16),
            pltpu.VMEM((groups, chips - 1, group * rows, width), BF16),
            pltpu.VMEM((groups, chips - 1, group * rows, width), BF16),
            pltpu.VMEM((window, width), F32),
            pltpu.VMEM((width, window), F32),
            dma((2 * comps,)),
            dma((5,)),
            dma((width // TILE,)),
            dma((pairs - 1,)),
            dma((pairs - 1,)),
            dma((groups, chips)),
            dma((groups, chips)),
            dma((groups, chips - 1)),
            dma((groups, chips - 1)),
        ],
        compiler_params=pltpu.CompilerParams(
            collective_id=0, has_side_effects=True, vmem_limit_bytes=56 * 2**20
        ),
        cost_estimate=pl.CostEstimate(
            flops=2 * block_len * columns * window,
            bytes_accessed=2 * block_len * columns + 4 * width * window,
            transcendentals=0,
        ),
    )(*operands)


def solution(mesh):
    return jax.shard_map(
        per_device,
        mesh=mesh,
        in_specs=(
            P("comp", "pair"),
            P(),
            P(("comp", "pair"), None),
            P(),
            P(),
            P(("pair", "comp"), None),
        ),
        out_specs=P(("pair", "comp"), None),
        check_vma=False,
    )
```

```python
import functools

import jax
import jax.numpy as jnp
from jax import lax
from jax.experimental import pallas as pl
from jax.experimental.pallas import tpu as pltpu
from jax.sharding import PartitionSpec as P

TILE = 128
LANES = 128
GROUP = 1
MESH = pl.DeviceIdType.MESH
F32 = jnp.float32
BF16 = jnp.bfloat16


def xor(a, b, bits):
    out = 0
    for i in range(bits):
        x, y = (a // 2**i) % 2, (b // 2**i) % 2
        out = out + 2**i * (x + y - 2 * x * y)
    return out


def kernel(
    comps, pairs, row_dev, group,
    d_hbm, w_hbm, list_hbm, val_hbm, cond_hbm, mask_hbm, out_hbm,
    d_v, w_ref, list_ref, val_ref, cond_ref, mask_ref,
    panel, own, core_out, core_in, chip_out, chip_in, acc, out_v,
    load_sem, small_sem, out_sem, pan_s, pan_r, core_s, core_r, chip_s, chip_r,
):
    c = lax.axis_index("comp")
    p = lax.axis_index("pair")
    chips = comps // 2
    chip_bits = chips.bit_length() - 1
    pair_bits = pairs.bit_length() - 1
    core, chip = c % 2, c // 2
    block_len = d_v.shape[0]
    width = d_v.shape[1] // comps
    rows = comps * row_dev
    groups = pairs // group

    def chip_at(m):
        return xor(chip, m, chip_bits)

    spans = [(b * width, LANES) for b in range(comps)]
    spans += [(b * width + LANES, width - LANES) for b in range(comps)]
    loads = [
        pltpu.make_async_copy(
            d_hbm.at[:, pl.ds(at, size)], d_v.at[:, pl.ds(at, size)], load_sem.at[i]
        )
        for i, (at, size) in enumerate(spans)
    ]
    small = [
        pltpu.make_async_copy(source, target, small_sem.at[i])
        for i, (source, target) in enumerate(
            [
                (w_hbm, w_ref),
                (list_hbm, list_ref),
                (val_hbm, val_ref),
                (cond_hbm, cond_ref),
                (mask_hbm, mask_ref),
            ]
        )
    ]
    for load in loads[:comps] + small + loads[comps:]:
        load.start()

    barrier = pltpu.get_barrier_semaphore()
    peers = [{"comp": 2 * chip + 1 - core, "pair": p}]
    peers += [{"comp": 2 * chip_at(m) + core, "pair": p} for m in range(1, chips)]
    peers += [{"comp": c, "pair": xor(p, k, pair_bits)} for k in range(1, pairs)]
    for peer in peers:
        pl.semaphore_signal(barrier, inc=1, device_id=peer, device_id_type=MESH)

    shape = (rows, comps * LANES)
    row = lax.broadcasted_iota(jnp.int32, shape, 0)
    col = lax.broadcasted_iota(jnp.int32, shape, 1)
    select = ((row // row_dev) * LANES + row % row_dev == col).astype(F32).astype(BF16)
    for load in loads[:comps] + small[:1]:
        load.wait()
    picked = jnp.concatenate([d_v[:, b * width : b * width + LANES] for b in range(comps)], axis=1)
    turned = lax.dot_general(select, picked, (((1,), (1,)), ((), ())), preferred_element_type=F32)
    per = block_len // LANES
    for i in range(per):
        cols = slice(i * LANES, (i + 1) * LANES)
        panel[0, :, cols] = (turned[:, cols] * w_ref[pl.ds(c * per + i, 1), :]).astype(BF16)

    pl.semaphore_wait(barrier, len(peers))

    def panel_copy(k):
        return pltpu.make_async_remote_copy(
            src_ref=panel.at[0],
            dst_ref=panel.at[k],
            send_sem=pan_s.at[k - 1],
            recv_sem=pan_r.at[k - 1],
            device_id={"comp": c, "pair": xor(p, k, pair_bits)},
            device_id_type=MESH,
        )

    for k in range(1, pairs):
        panel_copy(k).start()

    def core_copy(g, m):
        return pltpu.make_async_remote_copy(
            src_ref=core_out.at[g, m],
            dst_ref=core_in.at[g, m],
            send_sem=core_s.at[g, m],
            recv_sem=core_r.at[g, m],
            device_id={"comp": 2 * chip + 1 - core, "pair": p},
            device_id_type=MESH,
        )

    def chip_copy(g, m):
        return pltpu.make_async_remote_copy(
            src_ref=chip_out.at[g, m - 1],
            dst_ref=chip_in.at[g, m - 1],
            send_sem=chip_s.at[g, m - 1],
            recv_sem=chip_r.at[g, m - 1],
            device_id={"comp": 2 * chip_at(m) + core, "pair": p},
            device_id_type=MESH,
        )

    for load in small[1:]:
        load.wait()
    table = val_ref.shape
    place = lax.broadcasted_iota(jnp.int32, table, 0) * LANES
    place = place + lax.broadcasted_iota(jnp.int32, table, 1)
    tile = (row_dev, LANES)
    on_row = lax.broadcasted_iota(jnp.int32, tile, 0)
    on_col = lax.broadcasted_iota(jnp.int32, tile, 1)
    diagonal = jnp.zeros(tile, F32)
    for j in range(row_dev):
        up = jnp.where(place == list_ref[1, j], cond_ref[...], 0.0)
        down = jnp.where(place == list_ref[0, j], val_ref[...], 0.0)
        energy = jnp.sum(up, axis=(0, 1), keepdims=True) - jnp.sum(down, axis=(0, 1), keepdims=True)
        diagonal = jnp.where((on_row == j) & (on_col == j), energy, diagonal)

    for load in loads[comps:]:
        load.wait()

    def block(lhs, b):
        start = pl.multiple_of(b * width, width)
        return jnp.dot(lhs, d_v[:, pl.ds(start, width)], preferred_element_type=F32)

    def reduce(g):
        total = own[g]
        for m in range(1, chips):
            chip_copy(g, m).wait_recv()
            total = total + chip_in[g, m - 1].astype(F32)
        for i in range(group):
            s = xor(p, g * group + i, pair_bits)
            for b in range(comps):
                at = pl.ds(pl.multiple_of((b * pairs + s) * row_dev, row_dev), row_dev)
                first = i * rows + b * row_dev
                for t in range(width // TILE):
                    cols = slice(t * TILE, (t + 1) * TILE)
                    factor = 2.0 * mask_ref[t, b].astype(F32)
                    acc[at, cols] = total[first : first + row_dev, cols] * factor

    order = list(range(chips - 1, 0, -1)) + [0]
    steps = [(m, True) for m in order[:2]]
    for i, m in enumerate(order):
        steps.append((m, False))
        if i + 2 < chips:
            steps.append((order[i + 2], True))

    def phase(g, carry):
        for i in range(group):
            if i:
                panel_copy(g * group + i).wait_recv()
            else:

                @pl.when(g > 0)
                def _():
                    panel_copy(g * group).wait_recv()

        lhs = panel[pl.ds(g * group, group)].reshape(group * rows, block_len)
        for m, away in steps:
            if away:
                core_out[g, m] = block(lhs, 2 * chip_at(m) + 1 - core).astype(BF16)
                core_copy(g, m).start()
                continue
            part = block(lhs, 2 * chip_at(m) + core)
            core_copy(g, m).wait_recv()
            part = part + core_in[g, m].astype(F32)
            if m:
                chip_out[g, m - 1] = part.astype(BF16)
                chip_copy(g, m).start()
            else:
                own[g] = part

        @pl.when(g > 0)
        def _():
            reduce(g - 1)

        return carry

    lax.fori_loop(0, groups, phase, 0)
    reduce(groups - 1)

    at = pl.ds(pl.multiple_of((c * pairs + p) * row_dev, row_dev), row_dev)
    acc[at, :LANES] = acc[at, :LANES] + diagonal
    stores = []
    for t in range(width // TILE):
        cut = pl.ds(t * TILE, TILE)
        out_v[cut, :] = acc[:, t * TILE : (t + 1) * TILE].T
        stores.append(pltpu.make_async_copy(out_v.at[cut], out_hbm.at[cut], out_sem.at[t]))
        stores[-1].start()

    for k in range(1, pairs):
        panel_copy(k).wait_send()

    def drain(g, carry):
        for m in range(chips):
            core_copy(g, m).wait_send()
            if m:
                chip_copy(g, m).wait_send()
        return carry

    lax.fori_loop(0, groups, drain, 0)
    for store in stores:
        store.wait()


def per_device(densities, coulomb, pair_list, valence_energy, conduction_energy, tile_mask):
    comps = lax.axis_size("comp")
    pairs = lax.axis_size("pair")
    chips = comps // 2
    block_len, columns = densities.shape
    width = columns // comps
    row_dev = pair_list.shape[0]
    rows = comps * row_dev
    window = rows * pairs
    group = GROUP
    groups = pairs // group
    dma = pltpu.SemaphoreType.DMA
    operands = (
        densities,
        coulomb.reshape(-1, LANES),
        pair_list.T,
        valence_energy.reshape(-1, LANES),
        conduction_energy.reshape(-1, LANES),
        tile_mask,
    )
    _, w, pair, val, cond, mask = operands
    return pl.pallas_call(
        functools.partial(kernel, comps, pairs, row_dev, group),
        out_shape=jax.ShapeDtypeStruct((width, window), F32),
        in_specs=[pl.BlockSpec(memory_space=pl.ANY)] * 6,
        out_specs=pl.BlockSpec(memory_space=pl.ANY),
        scratch_shapes=[
            pltpu.VMEM((block_len, columns), BF16),
            pltpu.VMEM(w.shape, F32),
            pltpu.SMEM(pair.shape, jnp.int32),
            pltpu.VMEM(val.shape, F32),
            pltpu.VMEM(cond.shape, F32),
            pltpu.SMEM(mask.shape, jnp.int32),
            pltpu.VMEM((pairs, rows, block_len), BF16),
            pltpu.VMEM((groups, group * rows, width), F32),
            pltpu.VMEM((groups, chips, group * rows, width), BF16),
            pltpu.VMEM((groups, chips, group * rows, width), BF16),
            pltpu.VMEM((groups, chips - 1, group * rows, width), BF16),
            pltpu.VMEM((groups, chips - 1, group * rows, width), BF16),
            pltpu.VMEM((window, width), F32),
            pltpu.VMEM((width, window), F32),
            dma((2 * comps,)),
            dma((5,)),
            dma((width // TILE,)),
            dma((pairs - 1,)),
            dma((pairs - 1,)),
            dma((groups, chips)),
            dma((groups, chips)),
            dma((groups, chips - 1)),
            dma((groups, chips - 1)),
        ],
        compiler_params=pltpu.CompilerParams(
            collective_id=0, has_side_effects=True, vmem_limit_bytes=56 * 2**20
        ),
        cost_estimate=pl.CostEstimate(
            flops=2 * block_len * columns * window,
            bytes_accessed=2 * block_len * columns + 4 * width * window,
            transcendentals=0,
        ),
    )(*operands)


def solution(mesh):
    return jax.shard_map(
        per_device,
        mesh=mesh,
        in_specs=(
            P("comp", "pair"),
            P(),
            P(("comp", "pair"), None),
            P(),
            P(),
            P(("pair", "comp"), None),
        ),
        out_specs=P(("pair", "comp"), None),
        check_vma=False,
    )
```

```python
import functools

import jax
import jax.numpy as jnp
from jax import lax
from jax.experimental import pallas as pl
from jax.experimental.pallas import tpu as pltpu
from jax.sharding import PartitionSpec as P

TILE = 128
LANES = 128
GROUP = 2
HALVES = 2
MESH = pl.DeviceIdType.MESH
F32 = jnp.float32
BF16 = jnp.bfloat16


def xor(a, b, bits):
    out = 0
    for i in range(bits):
        x, y = (a // 2**i) % 2, (b // 2**i) % 2
        out = out + 2**i * (x + y - 2 * x * y)
    return out


def kernel(
    comps, pairs, row_dev, group,
    d_hbm, w_hbm, list_hbm, val_hbm, cond_hbm, mask_hbm, out_hbm,
    d_v, w_ref, list_ref, val_ref, cond_ref, mask_ref,
    panel, own, core_out, core_in, chip_out, chip_in, acc, out_v,
    load_sem, small_sem, out_sem, pan_s, pan_r, pass_s, core_s, core_r, chip_s, chip_r,
):
    c = lax.axis_index("comp")
    p = lax.axis_index("pair")
    chips = comps // 2
    chip_bits = chips.bit_length() - 1
    pair_bits = pairs.bit_length() - 1
    core, chip = c % 2, c // 2
    block_len = d_v.shape[0]
    width = d_v.shape[1] // comps
    rows = comps * row_dev
    groups = pairs // group
    half = block_len // HALVES
    middle = ((p + 1) // 2) % 2 == 1

    def chip_at(m):
        return xor(chip, m, chip_bits)

    spans = [(b * width, LANES) for b in range(comps)]
    spans += [(b * width + LANES, width - LANES) for b in range(comps)]
    loads = [
        pltpu.make_async_copy(
            d_hbm.at[:, pl.ds(at, size)], d_v.at[:, pl.ds(at, size)], load_sem.at[i]
        )
        for i, (at, size) in enumerate(spans)
    ]
    small = [
        pltpu.make_async_copy(source, target, small_sem.at[i])
        for i, (source, target) in enumerate(
            [
                (w_hbm, w_ref),
                (list_hbm, list_ref),
                (val_hbm, val_ref),
                (cond_hbm, cond_ref),
                (mask_hbm, mask_ref),
            ]
        )
    ]
    for load in loads[:comps] + small + loads[comps:]:
        load.start()

    barrier = pltpu.get_barrier_semaphore()
    peers = [{"comp": 2 * chip + 1 - core, "pair": p}]
    peers += [{"comp": 2 * chip_at(m) + core, "pair": p} for m in range(1, chips)]
    peers += [{"comp": c, "pair": xor(p, k, pair_bits)} for k in range(1, pairs)]
    for peer in peers:
        pl.semaphore_signal(barrier, inc=1, device_id=peer, device_id_type=MESH)

    shape = (rows, comps * LANES)
    row = lax.broadcasted_iota(jnp.int32, shape, 0)
    col = lax.broadcasted_iota(jnp.int32, shape, 1)
    select = ((row // row_dev) * LANES + row % row_dev == col).astype(F32).astype(BF16)
    for load in loads[:comps] + small[:1]:
        load.wait()
    picked = jnp.concatenate([d_v[:, b * width : b * width + LANES] for b in range(comps)], axis=1)
    turned = lax.dot_general(select, picked, (((1,), (1,)), ((), ())), preferred_element_type=F32)
    per = block_len // LANES
    for i in range(per):
        cols = slice(i * LANES, (i + 1) * LANES)
        h, at = divmod(i * LANES, half)
        weighted = turned[:, cols] * w_ref[pl.ds(c * per + i, 1), :]
        panel[h, 0, :, at : at + LANES] = weighted.astype(BF16)

    pl.semaphore_wait(barrier, len(peers))

    def panel_copy(k, h, source=0, to=None, sem=None):
        return pltpu.make_async_remote_copy(
            src_ref=panel.at[h, source],
            dst_ref=panel.at[h, k],
            send_sem=pan_s.at[k - 1, h] if sem is None else sem,
            recv_sem=pan_r.at[k - 1, h],
            device_id={"comp": c, "pair": xor(p, k if to is None else to, pair_bits)},
            device_id_type=MESH,
        )

    def pass_on(source, h):
        to, slot = {3: (1, 2), 1: (3, 2), 2: (1, 3)}[source]
        return panel_copy(slot, h, source, to, pass_s.at[source - 1, h])

    for h in range(HALVES):
        panel_copy(1, h).start()

        @pl.when(middle)
        def _():
            panel_copy(3, h).start()

    for k in range(4, pairs):
        for h in range(HALVES):
            panel_copy(k, h).start()

    def core_copy(g, m):
        return pltpu.make_async_remote_copy(
            src_ref=core_out.at[g, m],
            dst_ref=core_in.at[g, m],
            send_sem=core_s.at[g, m],
            recv_sem=core_r.at[g, m],
            device_id={"comp": 2 * chip + 1 - core, "pair": p},
            device_id_type=MESH,
        )

    def chip_copy(g, m):
        return pltpu.make_async_remote_copy(
            src_ref=chip_out.at[g, m - 1],
            dst_ref=chip_in.at[g, m - 1],
            send_sem=chip_s.at[g, m - 1],
            recv_sem=chip_r.at[g, m - 1],
            device_id={"comp": 2 * chip_at(m) + core, "pair": p},
            device_id_type=MESH,
        )

    for load in small[1:]:
        load.wait()
    table = val_ref.shape
    place = lax.broadcasted_iota(jnp.int32, table, 0) * LANES
    place = place + lax.broadcasted_iota(jnp.int32, table, 1)
    tile = (row_dev, LANES)
    on_row = lax.broadcasted_iota(jnp.int32, tile, 0)
    on_col = lax.broadcasted_iota(jnp.int32, tile, 1)
    diagonal = jnp.zeros(tile, F32)
    for j in range(row_dev):
        up = jnp.where(place == list_ref[1, j], cond_ref[...], 0.0)
        down = jnp.where(place == list_ref[0, j], val_ref[...], 0.0)
        energy = jnp.sum(up, axis=(0, 1), keepdims=True) - jnp.sum(down, axis=(0, 1), keepdims=True)
        diagonal = jnp.where((on_row == j) & (on_col == j), energy, diagonal)

    for load in loads[comps:]:
        load.wait()

    def block(lhs, b):
        start = pl.multiple_of(b * width, width)
        return jnp.dot(lhs, d_v[:, pl.ds(start, width)], preferred_element_type=F32)

    def reduce(g, t):
        cols = slice(t * TILE, (t + 1) * TILE)
        total = own[g, :, cols]
        for m in range(1, chips):
            total = total + chip_in[g, m - 1, :, cols].astype(F32)
        for i in range(group):
            s = xor(p, g * group + i, pair_bits)
            for b in range(comps):
                at = pl.ds(pl.multiple_of((b * pairs + s) * row_dev, row_dev), row_dev)
                first = i * rows + b * row_dev
                factor = 2.0 * mask_ref[t, b].astype(F32)
                acc[at, cols] = total[first : first + row_dev] * factor

    order = list(range(chips - 1, 0, -1)) + [0]
    steps = [(m, True) for m in order[:2]]
    for i, m in enumerate(order):
        steps.append((m, False))
        if i + 2 < chips:
            steps.append((order[i + 2], True))

    def phase(g, carry):
        @pl.when((g == 0) & middle)
        def _():
            for h in range(HALVES):
                for k in (3, 1):
                    panel_copy(k, h).wait_recv()
                    pass_on(k, h).start()

        @pl.when((g == 0) & jnp.logical_not(middle))
        def _():
            for h in range(HALVES):
                panel_copy(1, h).wait_recv()

        @pl.when((g == 1) & jnp.logical_not(middle))
        def _():
            for h in range(HALVES):
                panel_copy(2, h).wait_recv()
                panel_copy(3, h).wait_recv()

        @pl.when(g > 1)
        def _():
            for i in range(group):
                for h in range(HALVES):
                    panel_copy(g * group + i, h).wait_recv()

        lhs = jnp.concatenate(
            [
                panel[h, pl.ds(g * group, group)].reshape(group * rows, half)
                for h in range(HALVES)
            ],
            axis=1,
        )
        for m, away in steps:
            if away:
                core_out[g, m] = block(lhs, 2 * chip_at(m) + 1 - core).astype(BF16)
                core_copy(g, m).start()
                continue
            part = block(lhs, 2 * chip_at(m) + core)
            core_copy(g, m).wait_recv()
            part = part + core_in[g, m].astype(F32)
            if m:
                chip_out[g, m - 1] = part.astype(BF16)
                chip_copy(g, m).start()
            else:
                own[g] = part

        @pl.when((g == 0) & middle)
        def _():
            for h in range(HALVES):
                panel_copy(2, h).wait_recv()
                pass_on(2, h).start()

        @pl.when(g > 0)
        def _():
            for m in range(1, chips):
                chip_copy(g - 1, m).wait_recv()
            for t in range(width // TILE):
                reduce(g - 1, t)

        return carry

    lax.fori_loop(0, groups, phase, 0)
    for m in range(chips - 1, 0, -1):
        chip_copy(groups - 1, m).wait_recv()

    at = pl.ds(pl.multiple_of((c * pairs + p) * row_dev, row_dev), row_dev)
    stores = []
    for t in range(width // TILE):
        reduce(groups - 1, t)
        if t == 0:
            acc[at, :LANES] = acc[at, :LANES] + diagonal
        cut = pl.ds(t * TILE, TILE)
        out_v[cut, :] = acc[:, t * TILE : (t + 1) * TILE].T
        stores.append(pltpu.make_async_copy(out_v.at[cut], out_hbm.at[cut], out_sem.at[t]))
        stores[-1].start()

    for h in range(HALVES):
        panel_copy(1, h).wait_send()

        @pl.when(middle)
        def _():
            panel_copy(3, h).wait_send()
            for k in (3, 1, 2):
                pass_on(k, h).wait_send()

        for k in range(4, pairs):
            panel_copy(k, h).wait_send()

    def drain(g, carry):
        for m in range(chips):
            core_copy(g, m).wait_send()
            if m:
                chip_copy(g, m).wait_send()
        return carry

    lax.fori_loop(0, groups, drain, 0)
    for store in stores:
        store.wait()


def per_device(densities, coulomb, pair_list, valence_energy, conduction_energy, tile_mask):
    comps = lax.axis_size("comp")
    pairs = lax.axis_size("pair")
    chips = comps // 2
    block_len, columns = densities.shape
    width = columns // comps
    row_dev = pair_list.shape[0]
    rows = comps * row_dev
    window = rows * pairs
    group = GROUP
    groups = pairs // group
    dma = pltpu.SemaphoreType.DMA
    operands = (
        densities,
        coulomb.reshape(-1, LANES),
        pair_list.T,
        valence_energy.reshape(-1, LANES),
        conduction_energy.reshape(-1, LANES),
        tile_mask,
    )
    _, w, pair, val, cond, mask = operands
    return pl.pallas_call(
        functools.partial(kernel, comps, pairs, row_dev, group),
        out_shape=jax.ShapeDtypeStruct((width, window), F32),
        in_specs=[pl.BlockSpec(memory_space=pl.ANY)] * 6,
        out_specs=pl.BlockSpec(memory_space=pl.ANY),
        scratch_shapes=[
            pltpu.VMEM((block_len, columns), BF16),
            pltpu.VMEM(w.shape, F32),
            pltpu.SMEM(pair.shape, jnp.int32),
            pltpu.VMEM(val.shape, F32),
            pltpu.VMEM(cond.shape, F32),
            pltpu.SMEM(mask.shape, jnp.int32),
            pltpu.VMEM((HALVES, pairs, rows, block_len // HALVES), BF16),
            pltpu.VMEM((groups, group * rows, width), F32),
            pltpu.VMEM((groups, chips, group * rows, width), BF16),
            pltpu.VMEM((groups, chips, group * rows, width), BF16),
            pltpu.VMEM((groups, chips - 1, group * rows, width), BF16),
            pltpu.VMEM((groups, chips - 1, group * rows, width), BF16),
            pltpu.VMEM((window, width), F32),
            pltpu.VMEM((width, window), F32),
            dma((2 * comps,)),
            dma((5,)),
            dma((width // TILE,)),
            dma((pairs - 1, HALVES)),
            dma((pairs - 1, HALVES)),
            dma((3, HALVES)),
            dma((groups, chips)),
            dma((groups, chips)),
            dma((groups, chips - 1)),
            dma((groups, chips - 1)),
        ],
        compiler_params=pltpu.CompilerParams(
            collective_id=0, has_side_effects=True, vmem_limit_bytes=56 * 2**20
        ),
        cost_estimate=pl.CostEstimate(
            flops=2 * block_len * columns * window,
            bytes_accessed=2 * block_len * columns + 4 * width * window,
            transcendentals=0,
        ),
    )(*operands)


def solution(mesh):
    return jax.shard_map(
        per_device,
        mesh=mesh,
        in_specs=(
            P("comp", "pair"),
            P(),
            P(("comp", "pair"), None),
            P(),
            P(),
            P(("pair", "comp"), None),
        ),
        out_specs=P(("pair", "comp"), None),
        check_vma=False,
    )
```

```python
import functools

import jax
import jax.numpy as jnp
from jax import lax
from jax.experimental import pallas as pl
from jax.experimental.pallas import tpu as pltpu
from jax.sharding import PartitionSpec as P

TILE = 128
LANES = 128
GROUP = 2
HALVES = 2
MESH = pl.DeviceIdType.MESH
F32 = jnp.float32
BF16 = jnp.bfloat16


def xor(a, b, bits):
    out = 0
    for i in range(bits):
        x, y = (a // 2**i) % 2, (b // 2**i) % 2
        out = out + 2**i * (x + y - 2 * x * y)
    return out


def kernel(
    comps, pairs, row_dev, group,
    d_hbm, w_hbm, list_hbm, val_hbm, cond_hbm, mask_hbm, out_hbm,
    d_v, w_ref, list_ref, val_ref, cond_ref, mask_ref,
    panel, own, core_out, core_in, chip_out, chip_in, acc, out_v,
    load_sem, small_sem, out_sem, pan_s, pan_r, pass_s, core_s, core_r, chip_s, chip_r,
):
    c = lax.axis_index("comp")
    p = lax.axis_index("pair")
    chips = comps // 2
    chip_bits = chips.bit_length() - 1
    pair_bits = pairs.bit_length() - 1
    core, chip = c % 2, c // 2
    block_len = d_v.shape[0]
    width = d_v.shape[1] // comps
    rows = comps * row_dev
    groups = pairs // group
    half = block_len // HALVES
    middle = ((p + 1) // 2) % 2 == 1

    def chip_at(m):
        return xor(chip, m, chip_bits)

    spans = [(b * width, LANES) for b in range(comps)]
    spans += [(b * width + LANES, width - LANES) for b in range(comps)]
    loads = [
        pltpu.make_async_copy(
            d_hbm.at[:, pl.ds(at, size)], d_v.at[:, pl.ds(at, size)], load_sem.at[i]
        )
        for i, (at, size) in enumerate(spans)
    ]
    small = [
        pltpu.make_async_copy(source, target, small_sem.at[i])
        for i, (source, target) in enumerate(
            [
                (w_hbm, w_ref),
                (list_hbm, list_ref),
                (val_hbm, val_ref),
                (cond_hbm, cond_ref),
                (mask_hbm, mask_ref),
            ]
        )
    ]
    for load in loads[:comps] + small + loads[comps:]:
        load.start()

    barrier = pltpu.get_barrier_semaphore()
    peers = [{"comp": 2 * chip + 1 - core, "pair": p}]
    peers += [{"comp": 2 * chip_at(m) + core, "pair": p} for m in range(1, chips)]
    peers += [{"comp": c, "pair": xor(p, k, pair_bits)} for k in range(1, pairs)]
    for peer in peers:
        pl.semaphore_signal(barrier, inc=1, device_id=peer, device_id_type=MESH)

    shape = (rows, comps * LANES)
    row = lax.broadcasted_iota(jnp.int32, shape, 0)
    col = lax.broadcasted_iota(jnp.int32, shape, 1)
    select = ((row // row_dev) * LANES + row % row_dev == col).astype(F32).astype(BF16)
    for load in loads[:comps] + small[:1]:
        load.wait()
    picked = jnp.concatenate([d_v[:, b * width : b * width + LANES] for b in range(comps)], axis=1)
    turned = lax.dot_general(select, picked, (((1,), (1,)), ((), ())), preferred_element_type=F32)
    per = block_len // LANES
    for i in range(per):
        cols = slice(i * LANES, (i + 1) * LANES)
        h, at = divmod(i * LANES, half)
        weighted = turned[:, cols] * w_ref[pl.ds(c * per + i, 1), :]
        panel[h, 0, :, at : at + LANES] = weighted.astype(BF16)

    pl.semaphore_wait(barrier, len(peers))

    def panel_copy(k, h, source=0, to=None, sem=None):
        return pltpu.make_async_remote_copy(
            src_ref=panel.at[h, source],
            dst_ref=panel.at[h, k],
            send_sem=pan_s.at[k - 1, h] if sem is None else sem,
            recv_sem=pan_r.at[k - 1, h],
            device_id={"comp": c, "pair": xor(p, k if to is None else to, pair_bits)},
            device_id_type=MESH,
        )

    def pass_on(source, h):
        to, slot = {3: (1, 2), 2: (1, 3)}[source]
        return panel_copy(slot, h, source, to, pass_s.at[source - 2, h])

    for h in range(HALVES):
        panel_copy(1, h).start()

        @pl.when(middle)
        def _():
            panel_copy(3, h).start()

    @pl.when(jnp.logical_not(middle))
    def _():
        for h in range(HALVES):
            panel_copy(2, h).start()

    for k in range(4, pairs):
        for h in range(HALVES):
            panel_copy(k, h).start()

    def core_copy(g, m):
        return pltpu.make_async_remote_copy(
            src_ref=core_out.at[g, m],
            dst_ref=core_in.at[g, m],
            send_sem=core_s.at[g, m],
            recv_sem=core_r.at[g, m],
            device_id={"comp": 2 * chip + 1 - core, "pair": p},
            device_id_type=MESH,
        )

    def chip_copy(g, m):
        return pltpu.make_async_remote_copy(
            src_ref=chip_out.at[g, m - 1],
            dst_ref=chip_in.at[g, m - 1],
            send_sem=chip_s.at[g, m - 1],
            recv_sem=chip_r.at[g, m - 1],
            device_id={"comp": 2 * chip_at(m) + core, "pair": p},
            device_id_type=MESH,
        )

    for load in small[1:]:
        load.wait()
    table = val_ref.shape
    place = lax.broadcasted_iota(jnp.int32, table, 0) * LANES
    place = place + lax.broadcasted_iota(jnp.int32, table, 1)
    tile = (row_dev, LANES)
    on_row = lax.broadcasted_iota(jnp.int32, tile, 0)
    on_col = lax.broadcasted_iota(jnp.int32, tile, 1)
    diagonal = jnp.zeros(tile, F32)
    for j in range(row_dev):
        up = jnp.where(place == list_ref[1, j], cond_ref[...], 0.0)
        down = jnp.where(place == list_ref[0, j], val_ref[...], 0.0)
        energy = jnp.sum(up, axis=(0, 1), keepdims=True) - jnp.sum(down, axis=(0, 1), keepdims=True)
        diagonal = jnp.where((on_row == j) & (on_col == j), energy, diagonal)

    for load in loads[comps:]:
        load.wait()

    def block(lhs, b):
        start = pl.multiple_of(b * width, width)
        return jnp.dot(lhs, d_v[:, pl.ds(start, width)], preferred_element_type=F32)

    def reduce(g, t):
        cols = slice(t * TILE, (t + 1) * TILE)
        total = own[g, :, cols]
        for m in range(1, chips):
            total = total + chip_in[g, m - 1, :, cols].astype(F32)
        for i in range(group):
            s = xor(p, g * group + i, pair_bits)
            for b in range(comps):
                at = pl.ds(pl.multiple_of((b * pairs + s) * row_dev, row_dev), row_dev)
                first = i * rows + b * row_dev
                factor = 2.0 * mask_ref[t, b].astype(F32)
                acc[at, cols] = total[first : first + row_dev] * factor

    order = list(range(chips - 1, 0, -1)) + [0]
    steps = [(m, True) for m in order[:2]]
    for i, m in enumerate(order[:-1]):
        steps.append((m, False))
        if i + 3 < chips:
            steps.append((order[i + 2], True))
    steps += [(0, True), (0, False)]

    def phase(g, carry):
        @pl.when((g == 0) & middle)
        def _():
            for h in range(HALVES):
                panel_copy(3, h).wait_recv()
                pass_on(3, h).start()
            for h in range(HALVES):
                panel_copy(1, h).wait_recv()

        @pl.when((g == 0) & jnp.logical_not(middle))
        def _():
            for h in range(HALVES):
                panel_copy(1, h).wait_recv()

        @pl.when((g == 1) & jnp.logical_not(middle))
        def _():
            for h in range(HALVES):
                panel_copy(2, h).wait_recv()
                panel_copy(3, h).wait_recv()

        @pl.when(g > 1)
        def _():
            for i in range(group):
                for h in range(HALVES):
                    panel_copy(g * group + i, h).wait_recv()

        lhs = jnp.concatenate(
            [
                panel[h, pl.ds(g * group, group)].reshape(group * rows, half)
                for h in range(HALVES)
            ],
            axis=1,
        )
        for step, (m, away) in enumerate(steps):
            for h in range(HALVES):
                if step == 3 + 2 * h:

                    @pl.when((g == 0) & middle)
                    def _():
                        panel_copy(2, h).wait_recv()
                        pass_on(2, h).start()

            if away:
                core_out[g, m] = block(lhs, 2 * chip_at(m) + 1 - core).astype(BF16)
                core_copy(g, m).start()
                continue
            part = block(lhs, 2 * chip_at(m) + core)
            core_copy(g, m).wait_recv()
            part = part + core_in[g, m].astype(F32)
            if m:
                chip_out[g, m - 1] = part.astype(BF16)
                chip_copy(g, m).start()
            else:
                own[g] = part

        @pl.when(g > 0)
        def _():
            for m in range(1, chips):
                chip_copy(g - 1, m).wait_recv()
            for t in range(width // TILE):
                reduce(g - 1, t)

        return carry

    lax.fori_loop(0, groups, phase, 0)
    for m in range(chips - 1, 0, -1):
        chip_copy(groups - 1, m).wait_recv()

    at = pl.ds(pl.multiple_of((c * pairs + p) * row_dev, row_dev), row_dev)
    stores = []
    for t in range(width // TILE):
        reduce(groups - 1, t)
        if t == 0:
            acc[at, :LANES] = acc[at, :LANES] + diagonal
        cut = pl.ds(t * TILE, TILE)
        out_v[cut, :] = acc[:, t * TILE : (t + 1) * TILE].T
        stores.append(pltpu.make_async_copy(out_v.at[cut], out_hbm.at[cut], out_sem.at[t]))
        stores[-1].start()

    for h in range(HALVES):
        panel_copy(1, h).wait_send()

        @pl.when(middle)
        def _():
            panel_copy(3, h).wait_send()
            for k in (3, 2):
                pass_on(k, h).wait_send()

        @pl.when(jnp.logical_not(middle))
        def _():
            panel_copy(2, h).wait_send()

        for k in range(4, pairs):
            panel_copy(k, h).wait_send()

    def drain(g, carry):
        for m in range(chips):
            core_copy(g, m).wait_send()
            if m:
                chip_copy(g, m).wait_send()
        return carry

    lax.fori_loop(0, groups, drain, 0)
    for store in stores:
        store.wait()


def per_device(densities, coulomb, pair_list, valence_energy, conduction_energy, tile_mask):
    comps = lax.axis_size("comp")
    pairs = lax.axis_size("pair")
    chips = comps // 2
    block_len, columns = densities.shape
    width = columns // comps
    row_dev = pair_list.shape[0]
    rows = comps * row_dev
    window = rows * pairs
    group = GROUP
    groups = pairs // group
    dma = pltpu.SemaphoreType.DMA
    operands = (
        densities,
        coulomb.reshape(-1, LANES),
        pair_list.T,
        valence_energy.reshape(-1, LANES),
        conduction_energy.reshape(-1, LANES),
        tile_mask,
    )
    _, w, pair, val, cond, mask = operands
    return pl.pallas_call(
        functools.partial(kernel, comps, pairs, row_dev, group),
        out_shape=jax.ShapeDtypeStruct((width, window), F32),
        in_specs=[pl.BlockSpec(memory_space=pl.ANY)] * 6,
        out_specs=pl.BlockSpec(memory_space=pl.ANY),
        scratch_shapes=[
            pltpu.VMEM((block_len, columns), BF16),
            pltpu.VMEM(w.shape, F32),
            pltpu.SMEM(pair.shape, jnp.int32),
            pltpu.VMEM(val.shape, F32),
            pltpu.VMEM(cond.shape, F32),
            pltpu.SMEM(mask.shape, jnp.int32),
            pltpu.VMEM((HALVES, pairs, rows, block_len // HALVES), BF16),
            pltpu.VMEM((groups, group * rows, width), F32),
            pltpu.VMEM((groups, chips, group * rows, width), BF16),
            pltpu.VMEM((groups, chips, group * rows, width), BF16),
            pltpu.VMEM((groups, chips - 1, group * rows, width), BF16),
            pltpu.VMEM((groups, chips - 1, group * rows, width), BF16),
            pltpu.VMEM((window, width), F32),
            pltpu.VMEM((width, window), F32),
            dma((2 * comps,)),
            dma((5,)),
            dma((width // TILE,)),
            dma((pairs - 1, HALVES)),
            dma((pairs - 1, HALVES)),
            dma((2, HALVES)),
            dma((groups, chips)),
            dma((groups, chips)),
            dma((groups, chips - 1)),
            dma((groups, chips - 1)),
        ],
        compiler_params=pltpu.CompilerParams(
            collective_id=0, has_side_effects=True, vmem_limit_bytes=56 * 2**20
        ),
        cost_estimate=pl.CostEstimate(
            flops=2 * block_len * columns * window,
            bytes_accessed=2 * block_len * columns + 4 * width * window,
            transcendentals=0,
        ),
    )(*operands)


def solution(mesh):
    return jax.shard_map(
        per_device,
        mesh=mesh,
        in_specs=(
            P("comp", "pair"),
            P(),
            P(("comp", "pair"), None),
            P(),
            P(),
            P(("pair", "comp"), None),
        ),
        out_specs=P(("pair", "comp"), None),
        check_vma=False,
    )
```

```python
import functools

import jax
import jax.numpy as jnp
from jax import lax
from jax.experimental import pallas as pl
from jax.experimental.pallas import tpu as pltpu
from jax.sharding import PartitionSpec as P

TILE = 128
LANES = 128
GROUP = 2
HALVES = 2
MESH = pl.DeviceIdType.MESH
F32 = jnp.float32
BF16 = jnp.bfloat16


def xor(a, b, bits):
    out = 0
    for i in range(bits):
        x, y = (a // 2**i) % 2, (b // 2**i) % 2
        out = out + 2**i * (x + y - 2 * x * y)
    return out


def kernel(
    comps, pairs, row_dev, group,
    d_hbm, w_hbm, list_hbm, val_hbm, cond_hbm, mask_hbm, out_hbm,
    d_v, w_ref, list_ref, val_ref, cond_ref, mask_ref,
    panel, own, core_out, core_in, chip_out, chip_in, acc, out_v,
    load_sem, small_sem, out_sem, pan_s, pan_r, pass_s, core_s, core_r, chip_s, chip_r,
):
    c = lax.axis_index("comp")
    p = lax.axis_index("pair")
    chips = comps // 2
    chip_bits = chips.bit_length() - 1
    pair_bits = pairs.bit_length() - 1
    core, chip = c % 2, c // 2
    block_len = d_v.shape[0]
    width = d_v.shape[1] // comps
    rows = comps * row_dev
    groups = pairs // group
    half = block_len // HALVES
    middle = ((p + 1) // 2) % 2 == 1

    def chip_at(m):
        return xor(chip, m, chip_bits)

    spans = [(b * width, LANES) for b in range(comps)]
    spans += [(b * width + LANES, width - LANES) for b in range(comps)]
    loads = [
        pltpu.make_async_copy(
            d_hbm.at[:, pl.ds(at, size)], d_v.at[:, pl.ds(at, size)], load_sem.at[i]
        )
        for i, (at, size) in enumerate(spans)
    ]
    small = [
        pltpu.make_async_copy(source, target, small_sem.at[i])
        for i, (source, target) in enumerate(
            [
                (w_hbm, w_ref),
                (list_hbm, list_ref),
                (val_hbm, val_ref),
                (cond_hbm, cond_ref),
                (mask_hbm, mask_ref),
            ]
        )
    ]
    for load in loads[:comps] + small + loads[comps:]:
        load.start()

    barrier = pltpu.get_barrier_semaphore()
    peers = [{"comp": 2 * chip + 1 - core, "pair": p}]
    peers += [{"comp": 2 * chip_at(m) + core, "pair": p} for m in range(1, chips)]
    peers += [{"comp": c, "pair": xor(p, k, pair_bits)} for k in range(1, pairs)]
    for peer in peers:
        pl.semaphore_signal(barrier, inc=1, device_id=peer, device_id_type=MESH)

    row = lax.broadcasted_iota(jnp.int32, (rows, LANES), 0)
    col = lax.broadcasted_iota(jnp.int32, (rows, LANES), 1)
    select = (row == col).astype(F32).astype(BF16)
    lane = lax.broadcasted_iota(jnp.int32, (block_len, LANES), 1) // row_dev
    for load in loads[:comps] + small[:1]:
        load.wait()
    packed = d_v[:, :LANES].astype(F32)
    for b in range(1, comps):
        moved = pltpu.roll(d_v[:, b * width : b * width + LANES].astype(F32), b * row_dev, 1)
        packed = jnp.where(lane == b, moved, packed)
    picked = packed.astype(BF16)
    turned = lax.dot_general(select, picked, (((1,), (1,)), ((), ())), preferred_element_type=F32)
    per = block_len // LANES
    for i in range(per):
        cols = slice(i * LANES, (i + 1) * LANES)
        h, at = divmod(i * LANES, half)
        weighted = turned[:, cols] * w_ref[pl.ds(c * per + i, 1), :]
        panel[h, 0, :, at : at + LANES] = weighted.astype(BF16)

    pl.semaphore_wait(barrier, len(peers))

    def panel_copy(k, h, source=0, to=None, sem=None):
        return pltpu.make_async_remote_copy(
            src_ref=panel.at[h, source],
            dst_ref=panel.at[h, k],
            send_sem=pan_s.at[k - 1, h] if sem is None else sem,
            recv_sem=pan_r.at[k - 1, h],
            device_id={"comp": c, "pair": xor(p, k if to is None else to, pair_bits)},
            device_id_type=MESH,
        )

    def pass_on(source, h):
        to, slot = {3: (1, 2), 2: (1, 3)}[source]
        return panel_copy(slot, h, source, to, pass_s.at[source - 2, h])

    for h in range(HALVES):
        panel_copy(1, h).start()

        @pl.when(middle)
        def _():
            panel_copy(3, h).start()

    @pl.when(jnp.logical_not(middle))
    def _():
        for h in range(HALVES):
            panel_copy(2, h).start()

    for k in range(4, pairs):
        for h in range(HALVES):
            panel_copy(k, h).start()

    def core_copy(g, m):
        return pltpu.make_async_remote_copy(
            src_ref=core_out.at[g, m],
            dst_ref=core_in.at[g, m],
            send_sem=core_s.at[g, m],
            recv_sem=core_r.at[g, m],
            device_id={"comp": 2 * chip + 1 - core, "pair": p},
            device_id_type=MESH,
        )

    def chip_copy(g, m):
        return pltpu.make_async_remote_copy(
            src_ref=chip_out.at[g, m - 1],
            dst_ref=chip_in.at[g, m - 1],
            send_sem=chip_s.at[g, m - 1],
            recv_sem=chip_r.at[g, m - 1],
            device_id={"comp": 2 * chip_at(m) + core, "pair": p},
            device_id_type=MESH,
        )

    for load in small[1:]:
        load.wait()
    table = val_ref.shape
    place = lax.broadcasted_iota(jnp.int32, table, 0) * LANES
    place = place + lax.broadcasted_iota(jnp.int32, table, 1)
    tile = (row_dev, LANES)
    on_row = lax.broadcasted_iota(jnp.int32, tile, 0)
    on_col = lax.broadcasted_iota(jnp.int32, tile, 1)
    diagonal = jnp.zeros(tile, F32)
    for j in range(row_dev):
        up = jnp.where(place == list_ref[1, j], cond_ref[...], 0.0)
        down = jnp.where(place == list_ref[0, j], val_ref[...], 0.0)
        energy = jnp.sum(up, axis=(0, 1), keepdims=True) - jnp.sum(down, axis=(0, 1), keepdims=True)
        diagonal = jnp.where((on_row == j) & (on_col == j), energy, diagonal)

    for load in loads[comps:]:
        load.wait()

    def block(lhs, b):
        start = pl.multiple_of(b * width, width)
        return jnp.dot(lhs, d_v[:, pl.ds(start, width)], preferred_element_type=F32)

    def reduce(g, t):
        cols = slice(t * TILE, (t + 1) * TILE)
        total = own[g, :, cols]
        for m in range(1, chips):
            total = total + chip_in[g, m - 1, :, cols].astype(F32)
        for i in range(group):
            s = xor(p, g * group + i, pair_bits)
            for b in range(comps):
                at = pl.ds(pl.multiple_of((b * pairs + s) * row_dev, row_dev), row_dev)
                first = i * rows + b * row_dev
                factor = 2.0 * mask_ref[t, b].astype(F32)
                acc[at, cols] = total[first : first + row_dev] * factor

    order = list(range(chips - 1, 0, -1)) + [0]
    steps = [(m, True) for m in order[:2]]
    for i, m in enumerate(order[:-1]):
        steps.append((m, False))
        if i + 3 < chips:
            steps.append((order[i + 2], True))
    steps += [(0, True), (0, False)]

    def phase(g, carry):
        @pl.when((g == 0) & middle)
        def _():
            for h in range(HALVES):
                panel_copy(3, h).wait_recv()
                pass_on(3, h).start()
            for h in range(HALVES):
                panel_copy(1, h).wait_recv()

        @pl.when((g == 0) & jnp.logical_not(middle))
        def _():
            for h in range(HALVES):
                panel_copy(1, h).wait_recv()

        @pl.when((g == 1) & jnp.logical_not(middle))
        def _():
            for h in range(HALVES):
                panel_copy(2, h).wait_recv()
                panel_copy(3, h).wait_recv()

        @pl.when(g > 1)
        def _():
            for i in range(group):
                for h in range(HALVES):
                    panel_copy(g * group + i, h).wait_recv()

        lhs = jnp.concatenate(
            [
                panel[h, pl.ds(g * group, group)].reshape(group * rows, half)
                for h in range(HALVES)
            ],
            axis=1,
        )
        for step, (m, away) in enumerate(steps):
            for h in range(HALVES):
                if step == 3 + 2 * h:

                    @pl.when((g == 0) & middle)
                    def _():
                        panel_copy(2, h).wait_recv()
                        pass_on(2, h).start()

            if away:
                core_out[g, m] = block(lhs, 2 * chip_at(m) + 1 - core).astype(BF16)
                core_copy(g, m).start()
                continue
            part = block(lhs, 2 * chip_at(m) + core)
            core_copy(g, m).wait_recv()
            part = part + core_in[g, m].astype(F32)
            if m:
                chip_out[g, m - 1] = part.astype(BF16)
                chip_copy(g, m).start()
            else:
                own[g] = part

        @pl.when(g > 0)
        def _():
            for m in range(1, chips):
                chip_copy(g - 1, m).wait_recv()
            for t in range(width // TILE):
                reduce(g - 1, t)

        return carry

    lax.fori_loop(0, groups, phase, 0)
    for m in range(chips - 1, 0, -1):
        chip_copy(groups - 1, m).wait_recv()

    at = pl.ds(pl.multiple_of((c * pairs + p) * row_dev, row_dev), row_dev)
    stores = []
    for t in range(width // TILE):
        reduce(groups - 1, t)
        if t == 0:
            acc[at, :LANES] = acc[at, :LANES] + diagonal
        cut = pl.ds(t * TILE, TILE)
        out_v[cut, :] = acc[:, t * TILE : (t + 1) * TILE].T
        stores.append(pltpu.make_async_copy(out_v.at[cut], out_hbm.at[cut], out_sem.at[t]))
        stores[-1].start()

    for h in range(HALVES):
        panel_copy(1, h).wait_send()

        @pl.when(middle)
        def _():
            panel_copy(3, h).wait_send()
            for k in (3, 2):
                pass_on(k, h).wait_send()

        @pl.when(jnp.logical_not(middle))
        def _():
            panel_copy(2, h).wait_send()

        for k in range(4, pairs):
            panel_copy(k, h).wait_send()

    def drain(g, carry):
        for m in range(chips):
            core_copy(g, m).wait_send()
            if m:
                chip_copy(g, m).wait_send()
        return carry

    lax.fori_loop(0, groups, drain, 0)
    for store in stores:
        store.wait()


def per_device(densities, coulomb, pair_list, valence_energy, conduction_energy, tile_mask):
    comps = lax.axis_size("comp")
    pairs = lax.axis_size("pair")
    chips = comps // 2
    block_len, columns = densities.shape
    width = columns // comps
    row_dev = pair_list.shape[0]
    rows = comps * row_dev
    window = rows * pairs
    group = GROUP
    groups = pairs // group
    dma = pltpu.SemaphoreType.DMA
    operands = (
        densities,
        coulomb.reshape(-1, LANES),
        pair_list.T,
        valence_energy.reshape(-1, LANES),
        conduction_energy.reshape(-1, LANES),
        tile_mask,
    )
    _, w, pair, val, cond, mask = operands
    return pl.pallas_call(
        functools.partial(kernel, comps, pairs, row_dev, group),
        out_shape=jax.ShapeDtypeStruct((width, window), F32),
        in_specs=[pl.BlockSpec(memory_space=pl.ANY)] * 6,
        out_specs=pl.BlockSpec(memory_space=pl.ANY),
        scratch_shapes=[
            pltpu.VMEM((block_len, columns), BF16),
            pltpu.VMEM(w.shape, F32),
            pltpu.SMEM(pair.shape, jnp.int32),
            pltpu.VMEM(val.shape, F32),
            pltpu.VMEM(cond.shape, F32),
            pltpu.SMEM(mask.shape, jnp.int32),
            pltpu.VMEM((HALVES, pairs, rows, block_len // HALVES), BF16),
            pltpu.VMEM((groups, group * rows, width), F32),
            pltpu.VMEM((groups, chips, group * rows, width), BF16),
            pltpu.VMEM((groups, chips, group * rows, width), BF16),
            pltpu.VMEM((groups, chips - 1, group * rows, width), BF16),
            pltpu.VMEM((groups, chips - 1, group * rows, width), BF16),
            pltpu.VMEM((window, width), F32),
            pltpu.VMEM((width, window), F32),
            dma((2 * comps,)),
            dma((5,)),
            dma((width // TILE,)),
            dma((pairs - 1, HALVES)),
            dma((pairs - 1, HALVES)),
            dma((2, HALVES)),
            dma((groups, chips)),
            dma((groups, chips)),
            dma((groups, chips - 1)),
            dma((groups, chips - 1)),
        ],
        compiler_params=pltpu.CompilerParams(
            collective_id=0, has_side_effects=True, vmem_limit_bytes=56 * 2**20
        ),
        cost_estimate=pl.CostEstimate(
            flops=2 * block_len * columns * window,
            bytes_accessed=2 * block_len * columns + 4 * width * window,
            transcendentals=0,
        ),
    )(*operands)


def solution(mesh):
    return jax.shard_map(
        per_device,
        mesh=mesh,
        in_specs=(
            P("comp", "pair"),
            P(),
            P(("comp", "pair"), None),
            P(),
            P(),
            P(("pair", "comp"), None),
        ),
        out_specs=P(("pair", "comp"), None),
        check_vma=False,
    )
```
